32 devices in a mesh: row: 8 (over z, core), col: 4 (over y, x).
Axes of the slice: x: 2, y: 2, z: 4, core: 2. Of those that a mesh axis runs over, the one named last changes fastest.
Arguments:
- hessian_inverse: float32 [6656, 6656], P('row', 'col'), may hold values from -9 to 13, as said below
- weights: bfloat16 [16384, 6656], P('row', 'col'), may hold values from -6 to 6
- pruned: int32 [512], replicated, may hold values from 0 to 6655, as said below
Outputs:
- inverse_updated: float32 [6656, 6656], P('row', 'col')
- weights_updated: float32 [16384, 6656], P('row', 'col')
The draws below stay inside these ranges and needn't reach their ends.
Inputs may be any that keep to these rules, and one draw needn't show every extreme that they name: `pruned`: 512 distinct hidden units in increasing order; at most 256 of them fall in one column tile of 1664 consecutive units, and exactly 256 in some tile. `hessian_inverse`: symmetric positive definite.
All inputs are finite; a program needn't handle non-finite values.
Results may differ from the reference program's by a relative error of at most 0.0003.
Values may be sent and summed in bfloat16 or wider, within the bound.
A program may use at most 128 MiB of HBM per device.

```python
import math
import jax
import jax.numpy as jnp
from jax import lax

H = 6656
K = 512
ROWS = 16384
COL_TILES = 4
CAP = 256


shared_rank = 32


common_weight = 2.0


def draw_hessian_inverse(key, part):
    first, second, third = jax.random.split(jax.random.fold_in(key, 23), 3)
    noise = jax.random.truncated_normal(first, -4.0, 4.0, (H, H), jnp.float32)
    symmetric = (jnp.triu(noise) + jnp.triu(noise, 1).T) * (0.4 / math.sqrt(H))
    factors = jax.random.normal(second, (H, shared_rank), jnp.float32)
    lengths = jnp.sqrt(jnp.sum(factors * factors, axis=1, keepdims=True) / shared_rank + 1e-06)
    factors = factors / lengths
    common = jnp.dot(factors, factors.T, precision=lax.Precision.HIGHEST) / shared_rank
    core = jnp.eye(H, dtype=jnp.float32) + symmetric + common_weight * common
    logs = jax.random.uniform(third, (H,), jnp.float32, math.log(0.3), math.log(3.0))
    roots = jnp.exp(0.5 * logs)
    return roots[:, None] * core * roots[None, :]


def draw_pruned(key, part):
    width = H // COL_TILES
    first, second, third = jax.random.split(jax.random.fold_in(key, 11), 3)
    boost = jax.random.randint(first, (COL_TILES,), 0, 4)
    heavy = jax.random.randint(second, (), 0, COL_TILES)
    boost = jnp.where(jnp.arange(COL_TILES) == heavy, 4, boost)
    noise = jax.random.randint(third, (COL_TILES, width), 0, 1024)
    score = (boost[:, None] * 1024 + noise) * H + jnp.arange(H, dtype=jnp.int32).reshape(COL_TILES, width)
    cutoff = lax.top_k(score, CAP)[0][:, CAP - 1]
    score = jnp.where(score >= cutoff[:, None], score, -1).reshape(H)
    chosen = lax.top_k(score, K)[1]
    return jnp.sort(chosen).astype(jnp.int32)


def shard_levels(own_key, extent, pieces, smallest, high):
    def one(axis_at, shards_of):
        draws = jax.random.uniform(jax.random.fold_in(jax.random.fold_in(own_key, 6), axis_at), (shards_of,), jnp.float32, smallest / len(pieces), high / len(pieces))
        return jnp.repeat(jnp.exp(draws), extent[axis_at] // shards_of).reshape((-1,) + (1,) * (len(extent) - axis_at - 1))

    loudness = one(*pieces[0])
    for cut in pieces[1:]:
        loudness = loudness * one(*cut)
    return loudness


def centred(key, extent, deviation, most, pieces=(), held_as=jnp.bfloat16):
    values = deviation * jax.random.normal(key, extent, jnp.float32)
    if pieces:
        values = values * shard_levels(key, extent, pieces, -0.22, 0.18)
    return jnp.clip(values, -most, most).astype(held_as)


def setup_inputs(seed: int = 0) -> dict:
    key_list = jax.random.split(jax.random.key(seed), 4)
    return {
        "hessian_inverse": draw_hessian_inverse(jax.random.fold_in(key_list[3], 71), 0),
        "weights": centred(key_list[1], (ROWS, H), 1.0, 6.0, ((0, 8), (1, 4))),
        "pruned": draw_pruned(jax.random.fold_in(key_list[3], 71), 0),
    }


def reference(hessian_inverse, weights, pruned):
    high = lax.Precision.HIGHEST
    panel = jnp.take(hessian_inverse, pruned, axis=0)
    block = jnp.take(panel, pruned, axis=1)
    inverse_cols = jnp.take(hessian_inverse, pruned, axis=1)
    weight_cols = jnp.take(weights, pruned, axis=1).astype(jnp.float32)
    factor = jnp.linalg.cholesky(block)
    solved = jax.scipy.linalg.cho_solve((factor, True), panel)
    inverse_updated = hessian_inverse - jnp.dot(inverse_cols, solved, precision=high)
    hit = jnp.zeros((hessian_inverse.shape[0],), jnp.float32).at[pruned].set(1.0)
    keep = 1.0 - hit
    weights_updated = (weights.astype(jnp.float32) - jnp.dot(weight_cols, solved, precision=high)) * keep[None, :]
    return (inverse_updated, weights_updated)
```

```python
import functools

import jax
import jax.numpy as jnp
from jax import lax
from jax.experimental import pallas as pl
from jax.experimental.pallas import tpu as pltpu
from jax.sharding import PartitionSpec as P

HIGH = lax.Precision.HIGHEST
EDGE = 128
GROUP = 4
VMEM_LIMIT = 48 * 1024 * 1024


def dot(a, b):
    return jnp.dot(a, b, preferred_element_type=jnp.float32)


def split(x, terms):
    parts = []
    for _ in range(terms):
        part = lax.reduce_precision(x, 8, 7)
        parts.append(part.astype(jnp.bfloat16))
        x = x - part
    return parts


def pick_columns(x, pick):
    a, b, c = (dot(part, pick) for part in split(x, 3))
    return (c + b) + a


def pick_rows(pick, x):
    a, b, c = (dot(pick, part) for part in split(x, 3))
    return (c + b) + a


def sweep_tile(tiles):
    lane = lax.broadcasted_iota(jnp.int32, (8, EDGE), 1)
    sub = lax.broadcasted_iota(jnp.int32, (8, EDGE), 0)
    for first in range(0, EDGE, GROUP):
        home, base = first // 8, first % 8
        wide = (8, EDGE)
        rows, cells = [], []
        for s in range(GROUP):
            row = tiles[home][base + s : base + s + 1, :]
            cells.append([jnp.broadcast_to(row[:, first + t : first + t + 1], wide) for t in range(GROUP)])
            row = jnp.broadcast_to(row, wide)
            inside = (lane >= first) & (lane < first + GROUP)
            rows.append(jnp.where(inside, jnp.where(lane == first + s, -1.0, 0.0), row))
        for s in range(GROUP):
            inv = 1.0 / cells[s][s]
            rows[s] = rows[s] * inv
            for t in range(s + 1, GROUP):
                cells[s][t] = cells[s][t] * inv
            for u in range(GROUP):
                if u == s:
                    continue
                factor = cells[u][s]
                rows[u] = rows[u] - factor * rows[s]
                for t in range(s + 1, GROUP):
                    cells[u][t] = cells[u][t] - factor * cells[s][t]
        fresh = []
        for g, tile in enumerate(tiles):
            total = jnp.where((lane >= first) & (lane < first + GROUP), 0.0, tile)
            for s in range(GROUP):
                total = total - jnp.broadcast_to(tile[:, first + s : first + s + 1], wide) * rows[s]
            if g == home:
                for s in range(GROUP):
                    total = jnp.where(sub == base + s, rows[s], total)
            fresh.append(total)
        tiles = fresh
    return tiles


def inverse_kernel(block_ref, out_ref, work, tile_ref):
    size = block_ref.shape[0]
    work[...] = block_ref[...]

    def step(k, carry):
        at = pl.ds(pl.multiple_of(k * EDGE, EDGE), EDGE)
        tile = work[at, at]
        tiles = sweep_tile([tile[g * 8 : g * 8 + 8, :] for g in range(EDGE // 8)])
        for g, part in enumerate(tiles):
            tile_ref[g * 8 : g * 8 + 8, :] = part
        columns = work[:, at]
        work[at, :] = -jnp.dot(
            tile_ref[...], work[at, :], precision=HIGH, preferred_element_type=jnp.float32
        )
        work[at, at] = tile_ref[...]
        rows = work[at, :]
        work[:, at] = jnp.zeros_like(columns)
        work[...] = work[...] - jnp.dot(
            columns, rows, precision=HIGH, preferred_element_type=jnp.float32
        )
        work[at, :] = rows
        return carry

    lax.fori_loop(0, size // EDGE, step, 0)
    out_ref[...] = -work[...]


def invert(block):
    size = block.shape[0]
    return pl.pallas_call(
        inverse_kernel,
        out_shape=jax.ShapeDtypeStruct(block.shape, jnp.float32),
        in_specs=[pl.BlockSpec(memory_space=pltpu.VMEM)],
        out_specs=pl.BlockSpec(memory_space=pltpu.VMEM),
        scratch_shapes=[
            pltpu.VMEM((size, size), jnp.float32),
            pltpu.VMEM((EDGE, EDGE), jnp.float32),
        ],
        compiler_params=pltpu.CompilerParams(vmem_limit_bytes=VMEM_LIMIT),
        cost_estimate=pl.CostEstimate(
            flops=200 * size**3, bytes_accessed=8 * size * size, transcendentals=0
        ),
    )(block)


def solve_kernel(inverse_ref, panel_ref, high_ref, low_ref):
    solved = jnp.dot(
        inverse_ref[...], panel_ref[...], precision=HIGH, preferred_element_type=jnp.float32
    )
    high = solved.astype(jnp.bfloat16)
    high_ref[...] = high
    low_ref[...] = (solved - high.astype(jnp.float32)).astype(jnp.bfloat16)


def solve(inverse, panel):
    count, width = panel.shape
    out = pl.BlockSpec((EDGE, width), lambda i: (i, 0))
    return pl.pallas_call(
        solve_kernel,
        grid=(count // EDGE,),
        out_shape=[jax.ShapeDtypeStruct(panel.shape, jnp.bfloat16)] * 2,
        in_specs=[
            pl.BlockSpec((EDGE, count), lambda i: (i, 0)),
            pl.BlockSpec((count, width), lambda i: (0, 0)),
        ],
        out_specs=[out, out],
        compiler_params=pltpu.CompilerParams(vmem_limit_bytes=VMEM_LIMIT),
        cost_estimate=pl.CostEstimate(
            flops=12 * count * count * width, bytes_accessed=8 * count * width, transcendentals=0
        ),
    )(inverse, panel)


def weights_kernel(weights_ref, packed_ref, place_ref, high_ref, low_ref, keep_ref, out_ref):
    columns = dot(packed_ref[...], place_ref[...]).astype(jnp.bfloat16)
    change = dot(columns, low_ref[...]) + dot(columns, high_ref[...])
    out_ref[...] = (weights_ref[...].astype(jnp.float32) - change) * keep_ref[...]


def inverse_update_kernel(hessian_ref, packed_ref, place_ref, high_ref, low_ref, out_ref):
    packed = packed_ref[...]
    first = packed.astype(jnp.bfloat16)
    second = (packed - first.astype(jnp.float32)).astype(jnp.bfloat16)
    first = dot(first, place_ref[...]).astype(jnp.bfloat16)
    second = dot(second, place_ref[...]).astype(jnp.bfloat16)
    change = dot(second, high_ref[...]) + dot(first, low_ref[...])
    change = change + dot(first, high_ref[...])
    out_ref[...] = hessian_ref[...] - change


def row_tile(rows, most=256):
    return max(t for t in range(16, most + 1, 16) if rows % t == 0)


def update(kernel, matrix, packed, place, high, low, extra, passes):
    rows, width = matrix.shape
    tile = row_tile(rows)
    whole = lambda x: pl.BlockSpec(x.shape, lambda i: (0, 0))
    rowed = lambda x: pl.BlockSpec((tile, x.shape[1]), lambda i: (i, 0))
    return pl.pallas_call(
        kernel,
        grid=(rows // tile,),
        out_shape=jax.ShapeDtypeStruct(matrix.shape, jnp.float32),
        in_specs=[rowed(matrix), rowed(packed), whole(place), whole(high), whole(low)]
        + [whole(x) for x in extra],
        out_specs=rowed(matrix),
        compiler_params=pltpu.CompilerParams(vmem_limit_bytes=VMEM_LIMIT),
        cost_estimate=pl.CostEstimate(
            flops=2 * passes * rows * width * high.shape[0],
            bytes_accessed=8 * rows * width,
            transcendentals=0,
        ),
    )(matrix, packed, place, high, low, *extra)


def on_device(hessian_inverse, weights, pruned):
    tile_rows, tile_cols = hessian_inverse.shape
    count = pruned.shape[0]
    tiles = lax.axis_size("col")
    me = lax.axis_index("col")
    row_start = lax.axis_index("row") * tile_rows
    col_start = me * tile_cols
    row_pick = ((pruned - row_start)[:, None] == jnp.arange(tile_rows)[None, :]).astype(jnp.bfloat16)
    capacity = 2 * count // tiles
    owner = pruned // tile_cols
    tile_first = jnp.sum((pruned[None, :] < (owner * tile_cols)[:, None]).astype(jnp.int32), axis=1)
    rank = jnp.arange(count, dtype=jnp.int32) - tile_first
    position = owner * capacity + rank
    slots = jnp.arange(capacity, dtype=jnp.int32)
    mine = (position[:, None] - me * capacity) == slots[None, :]
    local = jnp.sum(jnp.where(mine, pruned[:, None] - col_start + 1, 0), axis=0) - 1
    slot_pick = (jnp.arange(tile_cols)[:, None] == local[None, :]).astype(jnp.bfloat16)
    place = (jnp.arange(tiles * capacity)[:, None] == position[None, :]).astype(jnp.bfloat16)

    packed_inverse = pick_columns(hessian_inverse, slot_pick)
    block_part = pick_rows(row_pick, packed_inverse)
    block_part = pick_columns(block_part, mine.T.astype(jnp.bfloat16))
    block = lax.psum(block_part, ("row", "col"))
    panel = lax.psum(pick_rows(row_pick, hessian_inverse), "row")
    packed_weights = dot(weights, slot_pick).astype(jnp.bfloat16)
    gathered_inverse = lax.all_gather(packed_inverse, "col", axis=1, tiled=True)
    gathered_weights = lax.all_gather(packed_weights, "col", axis=1, tiled=True)
    inverse = invert(block)
    high, low = solve(inverse, panel)
    hit = jnp.any((pruned - col_start)[:, None] == jnp.arange(tile_cols)[None, :], axis=0)
    keep = jnp.where(hit, 0.0, 1.0)[None, :]
    inverse_updated = update(
        inverse_update_kernel, hessian_inverse, gathered_inverse, place, high, low, (), 4
    )
    weights_updated = update(
        weights_kernel, weights, gathered_weights, place, high, low, (keep,), 3
    )
    return (inverse_updated, weights_updated)


def solution(mesh):
    in_specs = (P("row", "col"), P("row", "col"), P())
    out_specs = (P("row", "col"), P("row", "col"))
    return jax.shard_map(
        on_device, mesh=mesh, in_specs=in_specs, out_specs=out_specs, check_vma=False
    )
```
